32 devices in a mesh: ga: 8 (over y, x, core), ba: 4 (over z).
Axes of the slice: x: 2, y: 2, z: 4, core: 2. Of those that a mesh axis runs over, the one named last changes fastest.
Arguments:
- pairs: bfloat16 [48, 64, 4096], P('ba', None, 'ga'), may hold values from -0.059814453 to 0.059814453
- dielectric: bfloat16 [4, 4096, 4096], P(None, 'ga'), may hold values from -0.5 to 1.5, as said below
- freq_weight: float32 [4, 48], P(None, 'ba'), may hold values from 0.1 to 1
- shells: int32 [4096], P('ga'), may hold values from 0 to 63
Outputs:
- sigma: float32 [4, 64, 64], P(None, 'ba')
The draws below stay inside these ranges and needn't reach their ends.
Inputs may be any that keep to these rules, and one draw needn't show every extreme that they name: `dielectric`: each frequency's matrix is its diagonal plus small full-rank off-diagonal entries; the diagonal lies between 0.5 and 1.5.
All inputs are finite; a program needn't handle non-finite values.
Results may differ from the reference program's by a relative error of at most 0.0003.
Values may be sent and summed in bfloat16 or wider, within the bound.
A program may use at most 64 MiB of HBM per device.

```python
import math
import jax
import jax.numpy as jnp
from jax import lax

NG = 4096
NS = 64
NF = 4
NK = 48


def draw_dielectric(key, part):
    key = jax.random.fold_in(key, 11)
    first, second = jax.random.split(key)
    rough = jax.random.normal(first, (NF, NG, NG), jnp.float32) * (0.5 / NG ** 0.5)
    rough = jnp.clip(rough, -0.4, 0.4)
    diagonal = jax.random.uniform(second, (NF, NG), jnp.float32, 0.5, 1.5)
    eye = jnp.eye(NG, dtype=jnp.float32)
    return (rough * (1.0 - eye) + diagonal[:, :, None] * eye).astype(jnp.bfloat16)


def plant(entries, stream_key, least, high):
    longest = entries.shape.index(max(entries.shape))
    spots = []
    for shift in (0, 1):
        where = [jax.random.randint(jax.random.fold_in(stream_key, axis), (), 0, length) for axis, length in enumerate(entries.shape)]
        where[longest] = (where[longest] + shift) % entries.shape[longest]
        spots.append(tuple(where))
    return entries.at[spots[0]].set(least).at[spots[1]].set(high)


def level_of(own_key, dims, cuts, least, largest):
    gain = 1.0
    for position, blocks in cuts:
        draws = jax.random.uniform(jax.random.fold_in(jax.random.fold_in(own_key, 6), position), (blocks,), jnp.float32, least / len(cuts), largest / len(cuts))
        gain = gain * jnp.repeat(jnp.exp(draws), dims[position] // blocks).reshape((-1,) + (1,) * (len(dims) - 1 - position))
    return gain


def scatter_about(key, extent, scale, most, pieces=(), held_as=jnp.bfloat16):
    entries = scale * jax.random.normal(key, extent, jnp.float32)
    if pieces:
        entries = entries * level_of(key, extent, pieces, -0.22, 0.18)
    return jnp.clip(entries, -most, most).astype(held_as)


def setup_inputs(seed: int = 0) -> dict:
    keys = jax.random.split(jax.random.key(seed), 5)
    pairs = scatter_about(keys[0], (NK, NS, NG), 0.01, 0.059814453, ((0, 4), (2, 8)))
    dielectric = draw_dielectric(jax.random.fold_in(keys[4], 71), 0)
    freq_weight = jnp.clip(jnp.exp(math.log(1.0) - 2.3025851 * jax.random.uniform(keys[2], (NF, NK), jnp.float32) ** level_of(keys[2], (NF, NK), ((1, 4),), -0.2, 0.2)), 0.1, 1.0)
    shells = plant(jax.random.randint(keys[3], (NG,), 0, 64), jax.random.fold_in(keys[3], 1), 0, 63).astype(jnp.int32)
    return {"pairs": pairs, "dielectric": dielectric, "freq_weight": freq_weight, "shells": shells}


def reference(pairs, dielectric, freq_weight, shells):
    coulomb = lax.rsqrt(shells.astype(jnp.float32) + 1.0)
    scaled = (pairs.astype(jnp.float32) * coulomb).astype(jnp.bfloat16)
    scaled_wide = scaled.astype(jnp.float32)

    def one_frequency(inputs):
        matrix, weights = inputs
        proj = jnp.einsum('kng,gh->knh', scaled_wide, matrix.astype(jnp.float32), precision=lax.Precision.HIGHEST)
        proj = proj * weights[:, None, None]
        return jnp.einsum('knh,kmh->nm', proj, scaled_wide, precision=lax.Precision.HIGHEST)
    return lax.map(one_frequency, (dielectric, freq_weight))
```

```python
import functools

import jax
import jax.numpy as jnp
from jax import lax
from jax.experimental import pallas as pl
from jax.experimental.pallas import tpu as pltpu
from jax.sharding import PartitionSpec as P

MESH = pl.DeviceIdType.MESH
CHUNKS = 4
NT = (((1,), (1,)), ((), ()))
NN = (((1,), (0,)), ((), ()))


def local(pairs, dielectric, freq_weight, shells):
    coulomb = lax.rsqrt(shells.astype(jnp.float32) + 1.0)
    scaled = (pairs.astype(jnp.float32) * coulomb).astype(jnp.bfloat16)
    num_freq, local_rows, all_columns = dielectric.shape
    summed_bands, bands, own_width = scaled.shape
    row_matrix = dielectric.reshape(num_freq * local_rows, all_columns)
    piece = lax.all_gather(scaled, "ga", axis=2, tiled=True)
    count = piece.shape[2]
    flat_piece = piece.reshape(summed_bands * bands, count)
    applied = lax.dot_general(
        row_matrix, flat_piece, (((1,), (1,)), ((), ())), preferred_element_type=jnp.float32
    )
    applied = applied.reshape(num_freq, local_rows, summed_bands, bands)
    applied = applied * freq_weight[:, None, :, None]
    partial_value = jnp.einsum(
        "kng,fgkm->fnm", scaled.astype(jnp.float32), applied, precision=lax.Precision.HIGHEST
    )
    summed = lax.psum(partial_value, "ga")
    result = lax.psum_scatter(summed, "ba", scatter_dimension=1, tiled=True)
    return result


def kernel(
    pairs_hbm, d_hbm, w_ref, shells_ref, out_ref,
    raw, s, d, acc_a, hl, acc, acc_t, red_src, red_recv, red_all,
    pairs_sem, d_sem, send_sem, recv_sem, relay_send, red_send, red_rsem, all_send, all_rsem,
):
    num_k, bands, width = raw.shape
    num_freq = d.shape[1]
    num_ba = red_src.shape[0]
    per = num_k // CHUNKS
    a = lax.axis_index("ga")
    b = lax.axis_index("ba")
    y, x, c = a // 4, (a // 2) % 2, a % 2

    def partner(mask):
        py = 1 - y if mask & 4 else y
        px = 1 - x if mask & 2 else x
        pc = 1 - c if mask & 1 else c
        return py * 4 + px * 2 + pc

    relay_to = (y + (1 - c) * (1 - 2 * y)) * 4 + (x + c * (1 - 2 * x)) * 2 + c
    relay_slot = 2 + 2 * c

    pairs_copies = []
    for j in range(CHUNKS):
        copy = pltpu.make_async_copy(
            pairs_hbm.at[pl.ds(j * per, per)], raw.at[pl.ds(j * per, per)], pairs_sem.at[j]
        )
        copy.start()
        pairs_copies.append(copy)
    d_copies = {}
    for slot in (0, 1, 6, 7, 2, 4, 3, 5):
        columns = pl.ds(pl.multiple_of(partner(slot) * width, width), width)
        d_copies[slot] = pltpu.make_async_copy(d_hbm.at[:, :, columns], d.at[slot], d_sem.at[slot])
        d_copies[slot].start()

    barrier = pltpu.get_barrier_semaphore()
    for mask in range(1, 8):
        pl.semaphore_signal(barrier, inc=1, device_id={"ga": partner(mask)}, device_id_type=MESH)
    for step in range(1, num_ba):
        pl.semaphore_signal(
            barrier, inc=1, device_id={"ba": (b + step) % num_ba}, device_id_type=MESH
        )

    coulomb = lax.rsqrt(shells_ref[...].astype(jnp.float32) + 1.0)

    def scale(j):
        pairs_copies[j].wait()
        rows = pl.ds(j * per, per)
        wide = raw[rows].reshape(per * bands, width).astype(jnp.float32) * coulomb
        s[0, rows] = wide.astype(jnp.bfloat16).reshape(per, bands, width)

    def send(src_slot, mask, dst_slot, j, sem):
        rows = pl.ds(j * per, per)
        target = relay_to if mask is None else partner(mask)
        copy = pltpu.make_async_remote_copy(
            src_ref=s.at[src_slot, rows],
            dst_ref=s.at[dst_slot, rows],
            send_sem=sem,
            recv_sem=recv_sem.at[dst_slot, j],
            device_id={"ga": target},
            device_id_type=MESH,
        )
        copy.start()
        return copy

    started = []

    def forward(slot, mask, dst_slot, j):
        started.append(send(slot, mask, dst_slot, j, send_sem.at[dst_slot, j]))

    arrived = set()

    def wait(slot, j):
        if slot == 0 or (slot, j) in arrived:
            return
        arrived.add((slot, j))
        rows = pl.ds(j * per, per)
        pltpu.make_async_remote_copy(
            src_ref=s.at[slot, rows], dst_ref=s.at[slot, rows],
            send_sem=send_sem.at[slot, j], recv_sem=recv_sem.at[slot, j],
            device_id={"ga": partner(1)}, device_id_type=MESH,
        ).wait_recv()

    ready = set()

    def need(slot):
        if slot not in ready:
            ready.add(slot)
            d_copies[slot].wait()

    def arrive(j):
        wait(2, j)
        forward(2, 1, 3, j)
        wait(4, j)
        forward(relay_slot, None, 6, j)
        forward(4, 1, 5, j)

    def arrive_far(j):
        wait(6, j)
        forward(6, 1, 7, j)

    def apply_h(slots, first, parts):
        for slot in slots:
            need(slot)
        size = per * parts[1]
        start = parts[0] * per

        def body(f, carry):
            total = None
            for slot in slots:
                left = s[slot, pl.ds(start, size)].reshape(size * bands, width)
                term = lax.dot_general(left, d[slot, f], NT, preferred_element_type=jnp.float32)
                total = term if total is None else total + term
            total = total.reshape(size, bands, width)
            if first:
                acc_a[pl.ds(start, size), f] = total
            else:
                acc_a[pl.ds(start, size), f] += total
            return carry

        lax.fori_loop(0, num_freq, body, 0)

    def split(which, rows, f, wide):
        high = wide.astype(jnp.bfloat16)
        low = (wide - high.astype(jnp.float32)).astype(jnp.bfloat16)
        hl[which, rows, 0, f] = high
        hl[which, rows, 1, f] = low

    def apply_g(which, slot, half):
        need(slot)
        size = num_k // 2
        rows = pl.ds(half * size, size)

        def body(f, carry):
            wide = lax.dot_general(
                s[0, rows].reshape(size * bands, width), d[slot, f], NN,
                preferred_element_type=jnp.float32,
            )
            split(which, rows, f, wide.reshape(size, bands, width))
            return carry

        lax.fori_loop(0, num_freq, body, 0)

    def second(which, slot, target, j):
        def body(k, carry):
            left = hl[which, k].reshape(2 * num_freq * bands, width)
            both = lax.dot_general(left, s[slot, k], NT, preferred_element_type=jnp.float32)
            both = both.reshape(2, num_freq, bands, bands)
            both = both[0] + both[1]
            return tuple(carry[f] + w_ref[f, k] * both[f] for f in range(num_freq))

        terms = tuple(target[f] for f in range(num_freq))
        for k in range(j * per, (j + 1) * per):
            terms = body(k, terms)
        for f in range(num_freq):
            target[f] = terms[f]

    acc[...] = jnp.zeros_like(acc)
    acc_t[...] = jnp.zeros_like(acc_t)

    scale(0)
    pl.semaphore_wait(barrier, 7 + num_ba - 1)
    for j in range(CHUNKS):
        if j:
            scale(j)
        forward(0, 2, 2, j)
        forward(0, 4, 4, j)
        started.append(send(0, 1, 1, j, relay_send.at[j]))

    for j in range(CHUNKS):
        wait(1, j)
    apply_h((0, 1), True, (0, CHUNKS))
    arrive(0)
    apply_h((2, 4), False, (0, 1))
    apply_g(0, 6, 0)
    apply_g(0, 6, 1)
    arrive(1)
    wait(3, 0)
    wait(5, 0)
    apply_h((2, 4), False, (1, 1))
    apply_h((3, 5), False, (0, 1))
    apply_g(1, 7, 0)
    arrive(2)
    apply_g(1, 7, 1)
    wait(3, 1)
    wait(5, 1)
    apply_h((3, 5), False, (1, 1))
    arrive_far(0)
    apply_h((2, 4), False, (2, 1))
    arrive(3)
    wait(3, 2)
    wait(5, 2)
    apply_h((3, 5), False, (2, 1))
    arrive_far(1)
    apply_h((2, 4), False, (3, 1))
    wait(3, 3)
    wait(5, 3)
    apply_h((3, 5), False, (3, 1))
    for j in range(CHUNKS):
        rows = pl.ds(j * per, per)
        for f in range(num_freq):
            split(2, rows, f, acc_a[rows, f])
        second(2, 0, acc_t, j)
        if j == 1:
            second(0, 6, acc, 0)
            second(0, 6, acc, 1)
            arrive_far(2)
    wait(7, 0)
    second(1, 7, acc, 0)
    wait(7, 1)
    second(1, 7, acc, 1)
    second(0, 6, acc, 2)
    arrive_far(3)
    wait(7, 2)
    second(1, 7, acc, 2)
    second(0, 6, acc, 3)
    wait(7, 3)
    second(1, 7, acc, 3)

    piece = bands // num_ba
    for pair in range(num_freq // 2):
        first_f = acc[2 * pair] + acc_t[2 * pair].T
        second_f = acc[2 * pair + 1] + acc_t[2 * pair + 1].T
        both = jnp.concatenate([first_f, second_f], axis=1)
        red_src[:, pair] = both.reshape(num_ba, piece, 2 * bands)

    red_copies = []
    for step in range(1, num_ba):
        to = (b + step) % num_ba
        copy = pltpu.make_async_remote_copy(
            src_ref=red_src.at[to], dst_ref=red_recv.at[step - 1],
            send_sem=red_send.at[step - 1], recv_sem=red_rsem.at[step - 1],
            device_id={"ba": to}, device_id_type=MESH,
        )
        copy.start()
        red_copies.append(copy)
    total = red_src[b]
    for step, copy in enumerate(red_copies):
        copy.wait_recv()
        total = total + red_recv[step]
    red_all[a] = total
    all_copies = []
    for mask in range(1, 8):
        copy = pltpu.make_async_remote_copy(
            src_ref=red_all.at[a], dst_ref=red_all.at[a],
            send_sem=all_send.at[mask], recv_sem=all_rsem.at[mask],
            device_id={"ga": partner(mask)}, device_id_type=MESH,
        )
        copy.start()
        all_copies.append(copy)
    for mask, copy in enumerate(all_copies, 1):
        slot = partner(mask)
        pltpu.make_async_remote_copy(
            src_ref=red_all.at[slot], dst_ref=red_all.at[slot],
            send_sem=all_send.at[mask], recv_sem=all_rsem.at[mask],
            device_id={"ga": slot}, device_id_type=MESH,
        ).wait_recv()
    total = red_all[0]
    for other in range(1, 8):
        total = total + red_all[other]
    for pair in range(num_freq // 2):
        out_ref[2 * pair] = total[pair][:, :bands]
        out_ref[2 * pair + 1] = total[pair][:, bands:]
    for copy in started + red_copies + all_copies:
        copy.wait_send()


def fused(pairs, dielectric, freq_weight, shells, num_ba):
    num_k, bands, width = pairs.shape
    num_freq, rows, columns = dielectric.shape
    bf16, f32 = jnp.bfloat16, jnp.float32
    piece = bands // num_ba
    dma = pltpu.SemaphoreType.DMA
    return pl.pallas_call(
        kernel,
        out_shape=jax.ShapeDtypeStruct((num_freq, piece, bands), f32),
        in_specs=[
            pl.BlockSpec(memory_space=pl.ANY),
            pl.BlockSpec(memory_space=pl.ANY),
            pl.BlockSpec(memory_space=pltpu.SMEM),
            pl.BlockSpec(memory_space=pltpu.VMEM),
        ],
        out_specs=pl.BlockSpec(memory_space=pltpu.VMEM),
        scratch_shapes=[
            pltpu.VMEM((num_k, bands, width), bf16),
            pltpu.VMEM((8, num_k, bands, width), bf16),
            pltpu.VMEM((8, num_freq, rows, width), bf16),
            pltpu.VMEM((num_k, num_freq, bands, width), f32),
            pltpu.VMEM((3, num_k, 2, num_freq, bands, width), bf16),
            pltpu.VMEM((num_freq, bands, bands), f32),
            pltpu.VMEM((num_freq, bands, bands), f32),
            pltpu.VMEM((num_ba, num_freq // 2, piece, 2 * bands), f32),
            pltpu.VMEM((num_ba - 1, num_freq // 2, piece, 2 * bands), f32),
            pltpu.VMEM((8, num_freq // 2, piece, 2 * bands), f32),
            dma((CHUNKS,)),
            dma((8,)),
            dma((8, CHUNKS)),
            dma((8, CHUNKS)),
            dma((CHUNKS,)),
            dma((num_ba - 1,)),
            dma((num_ba - 1,)),
            dma((8,)),
            dma((8,)),
        ],
        compiler_params=pltpu.CompilerParams(
            collective_id=0, has_side_effects=True, vmem_limit_bytes=58 * 1024 * 1024
        ),
        cost_estimate=pl.CostEstimate(
            flops=2 * num_freq * rows * columns * num_k * bands,
            bytes_accessed=2 * num_freq * rows * columns,
            transcendentals=0,
        ),
    )(pairs, dielectric, freq_weight, shells.reshape(1, width))


def solution(mesh):
    in_specs = (P("ba", None, "ga"), P(None, "ga", None), P(None, "ba"), P("ga"))
    out_specs = P(None, "ba", None)
    num_ga, num_ba = mesh.shape["ga"], mesh.shape["ba"]

    def run(pairs, dielectric, freq_weight, shells):
        num_k, bands, width = pairs.shape
        num_freq = dielectric.shape[0]
        fits = num_ga == 8 and width % 128 == 0 and num_k % CHUNKS == 0
        fits = fits and num_freq % 2 == 0 and bands == 64 and bands % (8 * num_ba) == 0
        if fits:
            return fused(pairs, dielectric, freq_weight, shells, num_ba)
        return local(pairs, dielectric, freq_weight, shells)

    return jax.shard_map(run, mesh=mesh, in_specs=in_specs, out_specs=out_specs, check_vma=False)
```

```python
import functools

import jax
import jax.numpy as jnp
from jax import lax
from jax.experimental import pallas as pl
from jax.experimental.pallas import tpu as pltpu
from jax.sharding import PartitionSpec as P

MESH = pl.DeviceIdType.MESH
CHUNKS = 4
NT = (((1,), (1,)), ((), ()))
NN = (((1,), (0,)), ((), ()))


def local(pairs, dielectric, freq_weight, shells):
    coulomb = lax.rsqrt(shells.astype(jnp.float32) + 1.0)
    scaled = (pairs.astype(jnp.float32) * coulomb).astype(jnp.bfloat16)
    num_freq, local_rows, all_columns = dielectric.shape
    summed_bands, bands, own_width = scaled.shape
    row_matrix = dielectric.reshape(num_freq * local_rows, all_columns)
    piece = lax.all_gather(scaled, "ga", axis=2, tiled=True)
    count = piece.shape[2]
    flat_piece = piece.reshape(summed_bands * bands, count)
    applied = lax.dot_general(
        row_matrix, flat_piece, (((1,), (1,)), ((), ())), preferred_element_type=jnp.float32
    )
    applied = applied.reshape(num_freq, local_rows, summed_bands, bands)
    applied = applied * freq_weight[:, None, :, None]
    partial_value = jnp.einsum(
        "kng,fgkm->fnm", scaled.astype(jnp.float32), applied, precision=lax.Precision.HIGHEST
    )
    summed = lax.psum(partial_value, "ga")
    result = lax.psum_scatter(summed, "ba", scatter_dimension=1, tiled=True)
    return result


def kernel(
    pairs_hbm, d_hbm, w_ref, shells_ref, out_ref,
    raw, s, d, acc_a, hl, acc, red_src, red_recv, red_all,
    pairs_sem, d_sem, send_sem, recv_sem, relay_send, red_send, red_rsem, all_send, all_rsem,
):
    num_k, bands, width = raw.shape
    num_freq = d.shape[1]
    num_ba = red_src.shape[0]
    part = width // CHUNKS
    half = width // 2
    a = lax.axis_index("ga")
    b = lax.axis_index("ba")
    y, x, c = a // 4, (a // 2) % 2, a % 2

    def partner(mask):
        py = 1 - y if mask & 4 else y
        px = 1 - x if mask & 2 else x
        pc = 1 - c if mask & 1 else c
        return py * 4 + px * 2 + pc

    relay_to = (y + (1 - c) * (1 - 2 * y)) * 4 + (x + c * (1 - 2 * x)) * 2 + c
    relay_slot = 2 + 2 * c

    pairs_copies = []
    for j in range(CHUNKS):
        copy = pltpu.make_async_copy(
            pairs_hbm.at[:, :, pl.ds(j * part, part)],
            raw.at[:, :, pl.ds(j * part, part)],
            pairs_sem.at[j],
        )
        copy.start()
        pairs_copies.append(copy)
    d_copies = {}
    for slot in (6, 0, 1, 7, 2, 4, 3, 5):
        columns = pl.ds(pl.multiple_of(partner(slot) * width, width), width)
        d_copies[slot] = pltpu.make_async_copy(d_hbm.at[:, :, columns], d.at[slot], d_sem.at[slot])
        d_copies[slot].start()

    barrier = pltpu.get_barrier_semaphore()
    for mask in range(1, 8):
        pl.semaphore_signal(barrier, inc=1, device_id={"ga": partner(mask)}, device_id_type=MESH)
    for step in range(1, num_ba):
        pl.semaphore_signal(
            barrier, inc=1, device_id={"ba": (b + step) % num_ba}, device_id_type=MESH
        )

    coulomb = lax.rsqrt(shells_ref[...].astype(jnp.float32) + 1.0)

    def scale(j):
        pairs_copies[j].wait()
        columns = pl.ds(j * part, part)
        wide = raw[:, :, columns].reshape(num_k * bands, part).astype(jnp.float32)
        wide = wide * coulomb[:, j * part : (j + 1) * part]
        s[0, :, :, columns] = wide.astype(jnp.bfloat16).reshape(num_k, bands, part)

    def send(src_slot, mask, dst_slot, j, sem):
        columns = pl.ds(j * part, part)
        target = relay_to if mask is None else partner(mask)
        copy = pltpu.make_async_remote_copy(
            src_ref=s.at[src_slot, :, :, columns],
            dst_ref=s.at[dst_slot, :, :, columns],
            send_sem=sem,
            recv_sem=recv_sem.at[dst_slot, j],
            device_id={"ga": target},
            device_id_type=MESH,
        )
        copy.start()
        return copy

    started = []

    def forward(slot, mask, dst_slot, j):
        started.append(send(slot, mask, dst_slot, j, send_sem.at[dst_slot, j]))

    arrived = set()

    def wait(slot, j):
        if slot == 0 or (slot, j) in arrived:
            return
        arrived.add((slot, j))
        columns = pl.ds(j * part, part)
        pltpu.make_async_remote_copy(
            src_ref=s.at[slot, :, :, columns], dst_ref=s.at[slot, :, :, columns],
            send_sem=send_sem.at[slot, j], recv_sem=recv_sem.at[slot, j],
            device_id={"ga": partner(1)}, device_id_type=MESH,
        ).wait_recv()

    ready = set()

    def need(slot):
        if slot not in ready:
            ready.add(slot)
            d_copies[slot].wait()

    def arrive(j):
        wait(2, j)
        forward(2, 1, 3, j)
        wait(4, j)
        forward(relay_slot, None, 6, j)
        forward(4, 1, 5, j)

    def arrive_far(j):
        wait(6, j)
        forward(6, 1, 7, j)

    def apply_h(slots, start, size, freqs, first=False):
        for slot in slots:
            need(slot)
        columns = pl.ds(start, size)

        def body(f, carry):
            total = None
            for slot in slots:
                left = s[slot, :, :, columns].reshape(num_k * bands, size)
                term = lax.dot_general(
                    left, d[slot, f, :, columns], NT, preferred_element_type=jnp.float32
                )
                total = term if total is None else total + term
            total = total.reshape(num_k, bands, width)
            if first:
                acc_a[:, f] = total
            else:
                acc_a[:, f] += total
            return carry

        lax.fori_loop(*freqs, body, 0)

    def split(wide):
        high = wide.astype(jnp.bfloat16)
        return high, (wide - high.astype(jnp.float32)).astype(jnp.bfloat16)

    def apply_g(which, slot, freqs):
        need(slot)

        def body(f, carry):
            wide = lax.dot_general(
                s[0].reshape(num_k * bands, width), d[slot, f], NN,
                preferred_element_type=jnp.float32,
            )
            high, low = split(wide.reshape(num_k, bands, width))
            hl[which, :, 0, f] = high
            hl[which, :, 1, f] = low
            return carry

        lax.fori_loop(*freqs, body, 0)

    def add_second(terms, k, left, right):
        both = lax.dot_general(left, right, NT, preferred_element_type=jnp.float32)
        both = both.reshape(2, num_freq, bands, bands)
        both = both[0] + both[1]
        return tuple(terms[f] + w_ref[f, k] * both[f] for f in range(num_freq))

    def second(which, slot, start, size):
        terms = tuple(acc[f] for f in range(num_freq))
        columns = pl.ds(start, size)
        for k in range(num_k):
            left = hl[which, k, :, :, :, columns].reshape(2 * num_freq * bands, size)
            terms = add_second(terms, k, left, s[slot, k, :, columns])
        for f in range(num_freq):
            acc[f] = terms[f]

    def second_own():
        terms = tuple(jnp.zeros((bands, bands), jnp.float32) for f in range(num_freq))
        for k in range(num_k):
            high, low = split(acc_a[k].reshape(num_freq * bands, width))
            terms = add_second(terms, k, jnp.concatenate([high, low], axis=0), s[0, k])
        for f in range(num_freq):
            acc[f] = terms[f].T

    scale(0)
    pl.semaphore_wait(barrier, 7 + num_ba - 1)
    for j in range(CHUNKS):
        if j:
            scale(j)
        forward(0, 2, 2, j)
        forward(0, 4, 4, j)
        started.append(send(0, 1, 1, j, relay_send.at[j]))

    low_f, high_f = (0, num_freq // 2), (num_freq // 2, num_freq)
    every_f = (0, num_freq)
    apply_g(0, 6, every_f)
    for j in range(CHUNKS):
        wait(1, j)
    apply_h((0, 1), 0, width, low_f, True)
    arrive(0)
    apply_h((0, 1), 0, width, high_f, True)
    apply_g(1, 7, low_f)
    arrive(1)
    apply_g(1, 7, high_f)
    apply_h((2, 4), 0, half, every_f)
    for j in (0, 1):
        wait(3, j)
        wait(5, j)
    apply_h((3, 5), 0, half, low_f)
    arrive(2)
    apply_h((3, 5), 0, half, high_f)
    arrive_far(0)
    arrive(3)
    apply_h((2, 4), half, half, every_f)
    arrive_far(1)
    for j in (2, 3):
        wait(3, j)
        wait(5, j)
    apply_h((3, 5), half, half, every_f)
    second_own()
    arrive_far(2)
    second(0, 6, 0, half)
    for j in (0, 1):
        wait(7, j)
    second(1, 7, 0, half)
    arrive_far(3)
    second(0, 6, half, half)
    for j in (2, 3):
        wait(7, j)
    second(1, 7, half, half)

    piece = bands // num_ba
    for pair in range(num_freq // 2):
        first_f = acc[2 * pair]
        second_f = acc[2 * pair + 1]
        both = jnp.concatenate([first_f, second_f], axis=1)
        red_src[:, pair] = both.reshape(num_ba, piece, 2 * bands)

    red_copies = []
    for step in range(1, num_ba):
        to = (b + step) % num_ba
        copy = pltpu.make_async_remote_copy(
            src_ref=red_src.at[to], dst_ref=red_recv.at[step - 1],
            send_sem=red_send.at[step - 1], recv_sem=red_rsem.at[step - 1],
            device_id={"ba": to}, device_id_type=MESH,
        )
        copy.start()
        red_copies.append(copy)
    total = red_src[b]
    for step, copy in enumerate(red_copies):
        copy.wait_recv()
        total = total + red_recv[step]
    red_all[a] = total
    all_copies = []
    for mask in range(1, 8):
        copy = pltpu.make_async_remote_copy(
            src_ref=red_all.at[a], dst_ref=red_all.at[a],
            send_sem=all_send.at[mask], recv_sem=all_rsem.at[mask],
            device_id={"ga": partner(mask)}, device_id_type=MESH,
        )
        copy.start()
        all_copies.append(copy)
    for mask, copy in enumerate(all_copies, 1):
        slot = partner(mask)
        pltpu.make_async_remote_copy(
            src_ref=red_all.at[slot], dst_ref=red_all.at[slot],
            send_sem=all_send.at[mask], recv_sem=all_rsem.at[mask],
            device_id={"ga": slot}, device_id_type=MESH,
        ).wait_recv()
    total = red_all[0]
    for other in range(1, 8):
        total = total + red_all[other]
    for pair in range(num_freq // 2):
        out_ref[2 * pair] = total[pair][:, :bands]
        out_ref[2 * pair + 1] = total[pair][:, bands:]
    for copy in started + red_copies + all_copies:
        copy.wait_send()


def fused(pairs, dielectric, freq_weight, shells, num_ba):
    num_k, bands, width = pairs.shape
    num_freq, rows, columns = dielectric.shape
    bf16, f32 = jnp.bfloat16, jnp.float32
    piece = bands // num_ba
    dma = pltpu.SemaphoreType.DMA
    return pl.pallas_call(
        kernel,
        out_shape=jax.ShapeDtypeStruct((num_freq, piece, bands), f32),
        in_specs=[
            pl.BlockSpec(memory_space=pl.ANY),
            pl.BlockSpec(memory_space=pl.ANY),
            pl.BlockSpec(memory_space=pltpu.SMEM),
            pl.BlockSpec(memory_space=pltpu.VMEM),
        ],
        out_specs=pl.BlockSpec(memory_space=pltpu.VMEM),
        scratch_shapes=[
            pltpu.VMEM((num_k, bands, width), bf16),
            pltpu.VMEM((8, num_k, bands, width), bf16),
            pltpu.VMEM((8, num_freq, rows, width), bf16),
            pltpu.VMEM((num_k, num_freq, bands, width), f32),
            pltpu.VMEM((2, num_k, 2, num_freq, bands, width), bf16),
            pltpu.VMEM((num_freq, bands, bands), f32),
            pltpu.VMEM((num_ba, num_freq // 2, piece, 2 * bands), f32),
            pltpu.VMEM((num_ba - 1, num_freq // 2, piece, 2 * bands), f32),
            pltpu.VMEM((8, num_freq // 2, piece, 2 * bands), f32),
            dma((CHUNKS,)),
            dma((8,)),
            dma((8, CHUNKS)),
            dma((8, CHUNKS)),
            dma((CHUNKS,)),
            dma((num_ba - 1,)),
            dma((num_ba - 1,)),
            dma((8,)),
            dma((8,)),
        ],
        compiler_params=pltpu.CompilerParams(
            collective_id=0, has_side_effects=True, vmem_limit_bytes=58 * 1024 * 1024
        ),
        cost_estimate=pl.CostEstimate(
            flops=2 * num_freq * rows * columns * num_k * bands,
            bytes_accessed=2 * num_freq * rows * columns,
            transcendentals=0,
        ),
    )(pairs, dielectric, freq_weight, shells.reshape(1, width))


def solution(mesh):
    in_specs = (P("ba", None, "ga"), P(None, "ga", None), P(None, "ba"), P("ga"))
    out_specs = P(None, "ba", None)
    num_ga, num_ba = mesh.shape["ga"], mesh.shape["ba"]

    def run(pairs, dielectric, freq_weight, shells):
        num_k, bands, width = pairs.shape
        num_freq = dielectric.shape[0]
        fits = num_ga == 8 and width % (128 * CHUNKS) == 0
        fits = fits and num_freq % 2 == 0 and bands == 64 and bands % (8 * num_ba) == 0
        if fits:
            return fused(pairs, dielectric, freq_weight, shells, num_ba)
        return local(pairs, dielectric, freq_weight, shells)

    return jax.shard_map(run, mesh=mesh, in_specs=in_specs, out_specs=out_specs, check_vma=False)
```

```python
import functools

import jax
import jax.numpy as jnp
from jax import lax
from jax.experimental import pallas as pl
from jax.experimental.pallas import tpu as pltpu
from jax.sharding import PartitionSpec as P

MESH = pl.DeviceIdType.MESH
CHUNKS = 4
NT = (((1,), (1,)), ((), ()))
NN = (((1,), (0,)), ((), ()))


def local(pairs, dielectric, freq_weight, shells):
    coulomb = lax.rsqrt(shells.astype(jnp.float32) + 1.0)
    scaled = (pairs.astype(jnp.float32) * coulomb).astype(jnp.bfloat16)
    num_freq, local_rows, all_columns = dielectric.shape
    summed_bands, bands, own_width = scaled.shape
    row_matrix = dielectric.reshape(num_freq * local_rows, all_columns)
    piece = lax.all_gather(scaled, "ga", axis=2, tiled=True)
    count = piece.shape[2]
    flat_piece = piece.reshape(summed_bands * bands, count)
    applied = lax.dot_general(
        row_matrix, flat_piece, (((1,), (1,)), ((), ())), preferred_element_type=jnp.float32
    )
    applied = applied.reshape(num_freq, local_rows, summed_bands, bands)
    applied = applied * freq_weight[:, None, :, None]
    partial_value = jnp.einsum(
        "kng,fgkm->fnm", scaled.astype(jnp.float32), applied, precision=lax.Precision.HIGHEST
    )
    summed = lax.psum(partial_value, "ga")
    result = lax.psum_scatter(summed, "ba", scatter_dimension=1, tiled=True)
    return result


def kernel(
    pairs_hbm, d_hbm, w_ref, shells_ref, out_ref,
    raw, s, d, acc_a, hl, acc, red_src, red_recv, red_all,
    pairs_sem, d_sem, send_sem, recv_sem, relay_send, red_send, red_rsem, all_send, all_rsem,
):
    num_k, bands, width = raw.shape
    num_freq = d.shape[1]
    num_ba = red_src.shape[0]
    part = width // CHUNKS
    half = width // 2
    a = lax.axis_index("ga")
    b = lax.axis_index("ba")
    y, x, c = a // 4, (a // 2) % 2, a % 2

    def partner(mask):
        py = 1 - y if mask & 4 else y
        px = 1 - x if mask & 2 else x
        pc = 1 - c if mask & 1 else c
        return py * 4 + px * 2 + pc

    relay_to = (y + (1 - c) * (1 - 2 * y)) * 4 + (x + c * (1 - 2 * x)) * 2 + c
    relay_slot = 2 + 2 * c

    pairs_copies = []
    for j in range(CHUNKS):
        copy = pltpu.make_async_copy(
            pairs_hbm.at[:, :, pl.ds(j * part, part)],
            raw.at[:, :, pl.ds(j * part, part)],
            pairs_sem.at[j],
        )
        copy.start()
        pairs_copies.append(copy)
    d_copies = {}
    for slot in (6, 0, 1, 7, 2, 4, 3, 5):
        columns = pl.ds(pl.multiple_of(partner(slot) * width, width), width)
        d_copies[slot] = pltpu.make_async_copy(d_hbm.at[:, :, columns], d.at[slot], d_sem.at[slot])
        d_copies[slot].start()

    barrier = pltpu.get_barrier_semaphore()
    for mask in range(1, 8):
        pl.semaphore_signal(barrier, inc=1, device_id={"ga": partner(mask)}, device_id_type=MESH)
    for step in range(1, num_ba):
        pl.semaphore_signal(
            barrier, inc=1, device_id={"ba": (b + step) % num_ba}, device_id_type=MESH
        )

    coulomb = lax.rsqrt(shells_ref[...].astype(jnp.float32) + 1.0)

    def scale(j):
        pairs_copies[j].wait()
        columns = pl.ds(j * part, part)
        wide = raw[:, :, columns].reshape(num_k * bands, part).astype(jnp.float32)
        wide = wide * coulomb[:, j * part : (j + 1) * part]
        s[0, :, :, columns] = wide.astype(jnp.bfloat16).reshape(num_k, bands, part)

    def send(src_slot, mask, dst_slot, j, sem):
        columns = pl.ds(j * part, part)
        target = relay_to if mask is None else partner(mask)
        copy = pltpu.make_async_remote_copy(
            src_ref=s.at[src_slot, :, :, columns],
            dst_ref=s.at[dst_slot, :, :, columns],
            send_sem=sem,
            recv_sem=recv_sem.at[dst_slot, j],
            device_id={"ga": target},
            device_id_type=MESH,
        )
        copy.start()
        return copy

    started = []

    def forward(slot, mask, dst_slot, j):
        started.append(send(slot, mask, dst_slot, j, send_sem.at[dst_slot, j]))

    arrived = set()

    def wait(slot, j):
        if slot == 0 or (slot, j) in arrived:
            return
        arrived.add((slot, j))
        columns = pl.ds(j * part, part)
        pltpu.make_async_remote_copy(
            src_ref=s.at[slot, :, :, columns], dst_ref=s.at[slot, :, :, columns],
            send_sem=send_sem.at[slot, j], recv_sem=recv_sem.at[slot, j],
            device_id={"ga": partner(1)}, device_id_type=MESH,
        ).wait_recv()

    ready = set()

    def need(slot):
        if slot not in ready:
            ready.add(slot)
            d_copies[slot].wait()

    def arrive(j):
        wait(2, j)
        forward(2, 1, 3, j)
        wait(4, j)
        forward(relay_slot, None, 6, j)
        forward(4, 1, 5, j)

    def arrive_far(j):
        wait(6, j)
        forward(6, 1, 7, j)

    def apply_h(slots, start, size, freqs, first=False):
        for slot in slots:
            need(slot)
        columns = pl.ds(start, size)

        def body(f, carry):
            total = None
            for slot in slots:
                left = s[slot, :, :, columns].reshape(num_k * bands, size)
                term = lax.dot_general(
                    left, d[slot, f, :, columns], NT, preferred_element_type=jnp.float32
                )
                total = term if total is None else total + term
            total = total.reshape(num_k, bands, width)
            if first:
                acc_a[:, f] = total
            else:
                acc_a[:, f] += total
            return carry

        lax.fori_loop(*freqs, body, 0)

    def split(wide):
        high = wide.astype(jnp.bfloat16)
        return high, (wide - high.astype(jnp.float32)).astype(jnp.bfloat16)

    def apply_g(which, slot, freqs):
        need(slot)

        def body(f, carry):
            wide = lax.dot_general(
                s[0].reshape(num_k * bands, width), d[slot, f], NN,
                preferred_element_type=jnp.float32,
            )
            high, low = split(wide.reshape(num_k, bands, width))
            hl[which, :, 0, f] = high
            hl[which, :, 1, f] = low
            return carry

        lax.fori_loop(*freqs, body, 0)

    def add_second(terms, k, left, right):
        both = lax.dot_general(left, right, NT, preferred_element_type=jnp.float32)
        both = both.reshape(2, num_freq, bands, bands)
        both = both[0] + both[1]
        return tuple(terms[f] + w_ref[f, k] * both[f] for f in range(num_freq))

    def second(which, slot, start, size):
        terms = tuple(acc[f] for f in range(num_freq))
        columns = pl.ds(start, size)
        for k in range(num_k):
            left = hl[which, k, :, :, :, columns].reshape(2 * num_freq * bands, size)
            terms = add_second(terms, k, left, s[slot, k, :, columns])
        for f in range(num_freq):
            acc[f] = terms[f]

    def second_own():
        terms = tuple(jnp.zeros((bands, bands), jnp.float32) for f in range(num_freq))
        for k in range(num_k):
            high, low = split(acc_a[k].reshape(num_freq * bands, width))
            terms = add_second(terms, k, jnp.concatenate([high, low], axis=0), s[0, k])
        for f in range(num_freq):
            acc[f] = terms[f].T

    scale(0)
    pl.semaphore_wait(barrier, 7 + num_ba - 1)
    for j in range(CHUNKS):
        if j:
            scale(j)
        forward(0, 2, 2, j)
        forward(0, 4, 4, j)
        started.append(send(0, 1, 1, j, relay_send.at[j]))

    low_f, high_f = (0, num_freq // 2), (num_freq // 2, num_freq)
    every_f = (0, num_freq)
    apply_g(0, 6, every_f)
    for j in range(CHUNKS):
        wait(1, j)
    apply_h((0, 1), 0, width, low_f, True)
    arrive(0)
    apply_h((0, 1), 0, width, high_f, True)
    apply_g(1, 7, low_f)
    arrive(1)
    apply_g(1, 7, high_f)
    apply_h((2, 4), 0, half, every_f)
    for j in (0, 1):
        wait(3, j)
        wait(5, j)
    apply_h((3, 5), 0, half, low_f)
    arrive(2)
    apply_h((3, 5), 0, half, high_f)
    arrive_far(0)
    arrive(3)
    apply_h((2, 4), half, half, every_f)
    arrive_far(1)
    for j in (2, 3):
        wait(3, j)
        wait(5, j)
    apply_h((3, 5), half, half, every_f)
    arrive_far(2)
    second_own()
    arrive_far(3)
    second(0, 6, 0, width)
    for j in range(CHUNKS):
        wait(7, j)
    second(1, 7, 0, width)

    piece = bands // num_ba
    for pair in range(num_freq // 2):
        first_f = acc[2 * pair]
        second_f = acc[2 * pair + 1]
        both = jnp.concatenate([first_f, second_f], axis=1)
        red_src[:, pair] = both.reshape(num_ba, piece, 2 * bands)

    red_copies = []
    for step in range(1, num_ba):
        to = (b + step) % num_ba
        copy = pltpu.make_async_remote_copy(
            src_ref=red_src.at[to], dst_ref=red_recv.at[step - 1],
            send_sem=red_send.at[step - 1], recv_sem=red_rsem.at[step - 1],
            device_id={"ba": to}, device_id_type=MESH,
        )
        copy.start()
        red_copies.append(copy)
    total = red_src[b]
    for step, copy in enumerate(red_copies):
        copy.wait_recv()
        total = total + red_recv[step]
    red_all[a] = total
    all_copies = []
    for mask in range(1, 8):
        copy = pltpu.make_async_remote_copy(
            src_ref=red_all.at[a], dst_ref=red_all.at[a],
            send_sem=all_send.at[mask], recv_sem=all_rsem.at[mask],
            device_id={"ga": partner(mask)}, device_id_type=MESH,
        )
        copy.start()
        all_copies.append(copy)
    for mask, copy in enumerate(all_copies, 1):
        slot = partner(mask)
        pltpu.make_async_remote_copy(
            src_ref=red_all.at[slot], dst_ref=red_all.at[slot],
            send_sem=all_send.at[mask], recv_sem=all_rsem.at[mask],
            device_id={"ga": slot}, device_id_type=MESH,
        ).wait_recv()
    total = red_all[0]
    for other in range(1, 8):
        total = total + red_all[other]
    for pair in range(num_freq // 2):
        out_ref[2 * pair] = total[pair][:, :bands]
        out_ref[2 * pair + 1] = total[pair][:, bands:]
    for copy in started + red_copies + all_copies:
        copy.wait_send()


def fused(pairs, dielectric, freq_weight, shells, num_ba):
    num_k, bands, width = pairs.shape
    num_freq, rows, columns = dielectric.shape
    bf16, f32 = jnp.bfloat16, jnp.float32
    piece = bands // num_ba
    dma = pltpu.SemaphoreType.DMA
    return pl.pallas_call(
        kernel,
        out_shape=jax.ShapeDtypeStruct((num_freq, piece, bands), f32),
        in_specs=[
            pl.BlockSpec(memory_space=pl.ANY),
            pl.BlockSpec(memory_space=pl.ANY),
            pl.BlockSpec(memory_space=pltpu.SMEM),
            pl.BlockSpec(memory_space=pltpu.VMEM),
        ],
        out_specs=pl.BlockSpec(memory_space=pltpu.VMEM),
        scratch_shapes=[
            pltpu.VMEM((num_k, bands, width), bf16),
            pltpu.VMEM((8, num_k, bands, width), bf16),
            pltpu.VMEM((8, num_freq, rows, width), bf16),
            pltpu.VMEM((num_k, num_freq, bands, width), f32),
            pltpu.VMEM((2, num_k, 2, num_freq, bands, width), bf16),
            pltpu.VMEM((num_freq, bands, bands), f32),
            pltpu.VMEM((num_ba, num_freq // 2, piece, 2 * bands), f32),
            pltpu.VMEM((num_ba - 1, num_freq // 2, piece, 2 * bands), f32),
            pltpu.VMEM((8, num_freq // 2, piece, 2 * bands), f32),
            dma((CHUNKS,)),
            dma((8,)),
            dma((8, CHUNKS)),
            dma((8, CHUNKS)),
            dma((CHUNKS,)),
            dma((num_ba - 1,)),
            dma((num_ba - 1,)),
            dma((8,)),
            dma((8,)),
        ],
        compiler_params=pltpu.CompilerParams(
            collective_id=0, has_side_effects=True, vmem_limit_bytes=58 * 1024 * 1024
        ),
        cost_estimate=pl.CostEstimate(
            flops=2 * num_freq * rows * columns * num_k * bands,
            bytes_accessed=2 * num_freq * rows * columns,
            transcendentals=0,
        ),
    )(pairs, dielectric, freq_weight, shells.reshape(1, width))


def solution(mesh):
    in_specs = (P("ba", None, "ga"), P(None, "ga", None), P(None, "ba"), P("ga"))
    out_specs = P(None, "ba", None)
    num_ga, num_ba = mesh.shape["ga"], mesh.shape["ba"]

    def run(pairs, dielectric, freq_weight, shells):
        num_k, bands, width = pairs.shape
        num_freq = dielectric.shape[0]
        fits = num_ga == 8 and width % (128 * CHUNKS) == 0
        fits = fits and num_freq % 2 == 0 and bands == 64 and bands % (8 * num_ba) == 0
        if fits:
            return fused(pairs, dielectric, freq_weight, shells, num_ba)
        return local(pairs, dielectric, freq_weight, shells)

    return jax.shard_map(run, mesh=mesh, in_specs=in_specs, out_specs=out_specs, check_vma=False)
```
